256 devices in a mesh: row: 8 (over z_lo, core), col: 8 (over x, z_hi), depth: 4 (over y).
Axes of the slice: x: 4, y: 4, z: 8 (z_hi: 2, z_lo: 4; z = z_hi * 4 + z_lo), core: 2. Of those that a mesh axis runs over, the one named last changes fastest.
Arguments:
- tokens: bfloat16 [5120, 8192], P(('row', 'depth'), 'col'), may hold values from -6 to 6
- weight: bfloat16 [8192, 4096], P('row', 'col'), may hold values from -0.0625 to 0.0625
- cotangent: bfloat16 [5120, 4096], P(('row', 'depth'), 'col'), may hold values from -6 to 6
- master: float32 [8192, 4096], P(('row', 'depth'), 'col'), may hold values from -0.1 to 0.1
- first_moment: float32 [8192, 4096], P(('row', 'depth'), 'col'), may hold values from -6 to 6
- second_moment: float32 [8192, 4096], P(('row', 'depth'), 'col'), may hold values from 0.1 to 10
Outputs:
- queries: bfloat16 [5120, 4096], P(('row', 'depth'), 'col')
- token_grad: bfloat16 [5120, 8192], P(('row', 'depth'), 'col')
- new_master: float32 [8192, 4096], P(('row', 'depth'), 'col')
- new_first: float32 [8192, 4096], P(('row', 'depth'), 'col')
- new_second: float32 [8192, 4096], P(('row', 'depth'), 'col')
- new_weight: bfloat16 [8192, 4096], P('row', 'col')
The draws below stay inside these ranges and needn't reach their ends.
All inputs are finite; a program needn't handle non-finite values.
Results may differ from the reference program's by a relative error of at most 0.001.
Values may be sent and summed in bfloat16 or wider, within the bound.
No kernel may reach another device: no remote copies, remote signals or barrier semaphores. Data moves between devices by JAX's collectives and lax.ppermute only.
A program may use at most 128 MiB of HBM per device.

```python
import math
import jax
import jax.numpy as jnp

D = 8192
HQ = 4096
TOKENS = 5120


def strengthened(values, rng, source, target, blocks, factor):
    owner, partner = [(jnp.arange(values.shape[axis_at]) // (values.shape[axis_at] // blocks)).reshape([-1 if axis == axis_at else 1 for axis in range(values.ndim)]) for axis_at in (source, target)]
    chosen = jax.random.permutation(rng, blocks)[partner]
    strong = (owner == chosen) | (owner == (partner + blocks // 2) % blocks)
    return jnp.where(strong, factor * values, values)


def shard_levels(rng, dims, split, smallest, largest):
    def one(dim, blocks):
        heights = jax.random.uniform(jax.random.fold_in(jax.random.fold_in(rng, 6), dim), (blocks,), jnp.float32, smallest / len(split), largest / len(split))
        return jnp.repeat(jnp.exp(heights), dims[dim] // blocks).reshape((-1,) + (1,) * (len(dims) - dim - 1))

    gain = one(*split[0])
    for cut in split[1:]:
        gain = gain * one(*cut)
    return gain


def bell_draw(stream_key, dims, width, bound, shards=(), held_as=jnp.bfloat16):
    drawn = width * jax.random.normal(stream_key, dims, jnp.float32)
    if shards:
        drawn = drawn * shard_levels(stream_key, dims, shards, -0.22, 0.18)
    return jnp.clip(drawn, -bound, bound).astype(held_as)


def noise_with(key, shape, scale, reach, cuts, heavy, dtype=jnp.bfloat16):
    values = scale * jax.random.normal(key, shape, jnp.float32)
    if cuts:
        values = values * shard_levels(key, shape, cuts, -0.22, 0.18)
    return jnp.clip(strengthened(values, jax.random.fold_in(key, 3), *heavy), -reach, reach).astype(dtype)


def setup_inputs(seed: int = 0) -> dict:
    arg_keys = jax.random.split(jax.random.key(seed), 7)
    return {
        "tokens": noise_with(arg_keys[0], (TOKENS, D), 1.0, 6.0, ((0, 32), (1, 8)), (0, 1, 32, 2.75)),
        "weight": bell_draw(arg_keys[1], (D, HQ), D ** -0.5, 0.0625, ((0, 8), (1, 8))),
        "cotangent": bell_draw(arg_keys[2], (TOKENS, HQ), 1.0, 6.0, ((0, 32), (1, 8))),
        "master": jnp.clip(jax.random.uniform(arg_keys[3], (D, HQ), jnp.float32, -0.1, 0.1) * shard_levels(arg_keys[3], (D, HQ), ((0, 32), (1, 8)), -0.4, 0.0), -0.1, 0.1),
        "first_moment": bell_draw(arg_keys[4], (D, HQ), 1.0, 6.0, ((0, 32), (1, 8)), jnp.float32),
        "second_moment": jnp.clip(jnp.exp(math.log(10.0) - 4.6051702 * jax.random.uniform(arg_keys[5], (D, HQ), jnp.float32) ** shard_levels(arg_keys[5], (D, HQ), ((0, 32), (1, 8)), -0.2, 0.2)), 0.1, 10.0),
    }


beta_one = 0.9
beta_two = 0.95
learn_rate = 0.02
decay_rate = 0.1
adam_eps = 1e-08
bias_one = 1.0 - 0.9 ** 50
bias_two = 1.0 - 0.95 ** 50

def reference(tokens, weight, cotangent, master, first_moment, second_moment):
    queries = jnp.dot(tokens, weight, preferred_element_type=jnp.float32).astype(jnp.bfloat16)
    token_grad = jnp.dot(cotangent, weight.T, preferred_element_type=jnp.float32).astype(jnp.bfloat16)
    grad = jnp.dot(tokens.T, cotangent, preferred_element_type=jnp.float32) * (1.0 / math.sqrt(TOKENS))
    new_first = beta_one * first_moment + (1.0 - beta_one) * grad
    new_second = beta_two * second_moment + (1.0 - beta_two) * grad * grad
    step_value = new_first / bias_one / (jnp.sqrt(new_second / bias_two) + adam_eps)
    new_master = master - learn_rate * (step_value + decay_rate * master)
    new_weight = new_master.astype(jnp.bfloat16)
    return (queries, token_grad, new_master, new_first, new_second, new_weight)
```

```python
import math

import jax
import jax.numpy as jnp
from jax import lax
from jax.sharding import PartitionSpec as P

beta_one = 0.9
beta_two = 0.95
learn_rate = 0.02
decay_rate = 0.1
adam_eps = 1e-08
bias_one = 1.0 - 0.9**50
bias_two = 1.0 - 0.95**50

AXES = ("row", "col", "depth")
f32 = jnp.float32
bf16 = jnp.bfloat16


def moves(sizes, change):
    rows, cols, depths = sizes
    pairs = []
    for r in range(rows):
        for c in range(cols):
            for y in range(depths):
                zlo, core, x, zhi, yy = change(r // 2, r % 2, c // 2, c % 2, y)
                pairs.append(
                    (
                        (r * cols + c) * depths + y,
                        ((zlo * 2 + core) * cols + x * 2 + zhi) * depths + yy,
                    )
                )
    return pairs


def local(tokens, weight, cotangent, master, first_moment, second_moment):
    sizes = tuple(lax.axis_size(a) for a in AXES)
    nz, nx, ny = sizes[0] // 2, sizes[1] // 2, sizes[2]
    total_tokens = tokens.shape[0] * sizes[0] * sizes[2]
    grad_scale = 1.0 / math.sqrt(total_tokens)

    def send(value, change):
        return lax.ppermute(value, AXES, moves(sizes, change))

    def flip(value):
        return send(value, lambda zlo, core, x, zhi, y: (x, zhi, zlo, core, y))

    def along_x(value, step):
        return send(value, lambda zlo, core, x, zhi, y: (zlo, core, (x + step) % nx, zhi, y))

    def along_z(value, step):
        return send(value, lambda zlo, core, x, zhi, y: ((zlo + step) % nz, core, x, zhi, y))

    def other_core(value):
        return send(value, lambda zlo, core, x, zhi, y: (zlo, 1 - core, x, zhi, y))

    def other_zhi(value):
        return send(value, lambda zlo, core, x, zhi, y: (zlo, core, x, 1 - zhi, y))

    row, col, y = (lax.axis_index(a) for a in AXES)
    zlo, core, x, zhi = row // 2, row % 2, col // 2, col % 2

    def over_col(value):
        far = other_zhi(value)
        pair = jnp.where(zhi == 0, jnp.stack([value, far]), jnp.stack([far, value]))
        left, right = along_x(pair, 1), along_x(pair, -1)
        across = jnp.stack([along_x(left[0], 1), along_x(right[1], -1)])
        whole = jnp.zeros((nx,) + pair.shape, pair.dtype)
        for step, block in ((0, pair), (1, left), (2, across), (3, right)):
            whole = lax.dynamic_update_index_in_dim(whole, block, (x - step) % nx, 0)
        return whole

    quarter = weight.shape[0] // ny
    part = lax.dynamic_slice_in_dim(weight, y * quarter, quarter, 0)

    turned_tokens = lax.all_to_all(flip(tokens), "depth", 1, 0, tiled=True)
    turned_part = flip(part)
    cot_parts = [cotangent] + [along_z(cotangent, s) for s in range(1, nz)]
    both = jnp.stack([part, turned_part])
    parts = [turned_part] + [along_z(both, s) for s in range(1, nz)]

    wide = over_col(jnp.concatenate([tokens, cotangent], axis=1))
    features = tokens.shape[1]
    turned = over_col(turned_tokens)

    def select(buffer, zl, co):
        return lax.dynamic_slice(
            buffer, (zl, co) + (0,) * (buffer.ndim - 2), (1, 1) + buffer.shape[2:]
        ).reshape(buffer.shape[2:])

    grad = 0.0
    for s in range(nz):
        mine = lax.all_gather(cot_parts[s], "depth", axis=0, tiled=True)
        theirs = other_core(mine)
        zl = (zlo - s) % nz
        for co, block in ((core, mine), (1 - core, theirs)):
            grad += lax.dot_general(
                select(turned, zl, co), block, (((0,), (0,)), ((), ())), preferred_element_type=f32
            )
    grad = grad * grad_scale
    new_first = beta_one * first_moment + (1.0 - beta_one) * grad
    new_second = beta_two * second_moment + (1.0 - beta_two) * grad * grad
    step_value = new_first / bias_one / (jnp.sqrt(new_second / bias_two) + adam_eps)
    new_master = master - learn_rate * (step_value + decay_rate * master)
    shard_weight = new_master.astype(bf16)
    new_weight = lax.all_gather(shard_weight, "depth", axis=0, tiled=True)

    queries = 0.0
    token_grad = 0.0
    for s in range(nz):
        gathered = lax.all_gather(parts[s], "depth", axis=0, tiled=False)
        if s == 0:
            mine = (weight, gathered.reshape(weight.shape))
            theirs = tuple(other_core(m) for m in mine)
        else:
            swapped = other_core(gathered)
            mine, theirs = (
                tuple(v[:, i].reshape(weight.shape) for i in range(2)) for v in (gathered, swapped)
            )
        zl = (zlo - s) % nz
        for co, (plain, turn) in ((core, mine), (1 - core, theirs)):
            block = select(wide, zl, co)
            queries += jnp.dot(block[:, :features], plain, preferred_element_type=f32)
            token_grad += lax.dot_general(
                block[:, features:], turn, (((1,), (1,)), ((), ())), preferred_element_type=f32
            )
    return (
        queries.astype(bf16),
        token_grad.astype(bf16),
        new_master,
        new_first,
        new_second,
        new_weight,
    )


def solution(mesh):
    in_specs = (
        P(("row", "depth"), "col"),
        P("row", "col"),
        P(("row", "depth"), "col"),
        P(("row", "depth"), "col"),
        P(("row", "depth"), "col"),
        P(("row", "depth"), "col"),
    )
    out_specs = (
        P(("row", "depth"), "col"),
        P(("row", "depth"), "col"),
        P(("row", "depth"), "col"),
        P(("row", "depth"), "col"),
        P(("row", "depth"), "col"),
        P("row", "col"),
    )
    return jax.shard_map(local, mesh=mesh, in_specs=in_specs, out_specs=out_specs, check_vma=False)
```

```python
import math

import jax
import jax.numpy as jnp
from jax import lax
from jax.sharding import PartitionSpec as P

beta_one = 0.9
beta_two = 0.95
learn_rate = 0.02
decay_rate = 0.1
adam_eps = 1e-08
bias_one = 1.0 - 0.9**50
bias_two = 1.0 - 0.95**50

AXES = ("row", "col", "depth")
f32 = jnp.float32
bf16 = jnp.bfloat16


def moves(sizes, change):
    rows, cols, depths = sizes
    pairs = []
    for r in range(rows):
        for c in range(cols):
            for y in range(depths):
                zlo, core, x, zhi, yy = change(r // 2, r % 2, c // 2, c % 2, y)
                pairs.append(
                    (
                        (r * cols + c) * depths + y,
                        ((zlo * 2 + core) * cols + x * 2 + zhi) * depths + yy,
                    )
                )
    return pairs


class Held:
    def __init__(self, value):
        self.value = value


class Lane:
    def __init__(self, lag):
        self.lag = lag
        self.past = []

    def send(self, held, pairs):
        if len(self.past) >= self.lag:
            before = self.past[-self.lag]
            if before is held:
                held.value = lax.optimization_barrier(held.value)
            else:
                held.value, before.value = lax.optimization_barrier((held.value, before.value))
        out = Held(lax.ppermute(held.value, AXES, pairs))
        self.past.append(out)
        return out


def local(tokens, weight, cotangent, master, first_moment, second_moment):
    sizes = tuple(lax.axis_size(a) for a in AXES)
    nz, nx, ny = sizes[0] // 2, sizes[1] // 2, sizes[2]
    total_tokens = tokens.shape[0] * sizes[0] * sizes[2]
    grad_scale = 1.0 / math.sqrt(total_tokens)
    row, col, y = (lax.axis_index(a) for a in AXES)
    zlo, core, x, zhi = row // 2, row % 2, col // 2, col % 2
    way = 1 - 2 * core

    def pairs(change):
        return moves(sizes, change)

    ring_x = pairs(lambda zl, co, xx, zh, yy: (zl, co, (xx + 1 - 2 * co) % nx, zh, yy))
    ring_y = pairs(lambda zl, co, xx, zh, yy: (zl, co, xx, zh, (yy + 1 - 2 * co) % ny))
    ring_z = pairs(lambda zl, co, xx, zh, yy: ((zl + 1 - 2 * co) % nz, co, xx, zh, yy))
    turn = pairs(lambda zl, co, xx, zh, yy: (xx, zh, zl, co, yy))
    turn_across = pairs(lambda zl, co, xx, zh, yy: (xx, zh, zl, 1 - co, yy))
    swap_core = pairs(lambda zl, co, xx, zh, yy: (zl, 1 - co, xx, zh, yy))
    swap_half = pairs(lambda zl, co, xx, zh, yy: (zl, co, xx, 1 - zh, yy))

    lane_x, lane_y, lane_z, lane_core = Lane(1), Lane(2), Lane(2), Lane(2)

    quarter = weight.shape[0] // ny
    rows = cotangent.shape[0]
    features = tokens.shape[1]
    part = Held(lax.dynamic_slice_in_dim(weight, y * quarter, quarter, 0))
    wide = Held(jnp.concatenate([tokens, cotangent], axis=1))
    token_block = Held(tokens)
    cot_block = Held(cotangent)
    spread = Held(lax.all_to_all(tokens, "depth", 1, 0, tiled=True))

    own_k = [wide]
    turned_part = lane_z.send(part, turn)
    cot_line = [cot_block]
    cot_line.append(lane_z.send(cot_line[-1], ring_z))
    own_k.append(lane_x.send(own_k[-1], ring_x))
    turned = [lane_z.send(spread, turn)]
    cot_line.append(lane_z.send(cot_line[-1], ring_z))
    own_k.append(lane_x.send(own_k[-1], ring_x))
    turned.append(lane_z.send(spread, turn_across))
    cot_line.append(lane_z.send(cot_line[-1], ring_z))
    own_k.append(lane_x.send(own_k[-1], ring_x))

    def gather_y(held):
        return [held]

    def step_y(blocks):
        blocks.append(lane_y.send(blocks[-1], ring_y))

    turned_y = [turned_part]
    cot_y = [Held(jnp.concatenate([c.value for c in cot_line], axis=0))]
    for _ in range(ny - 1):
        step_y(turned_y)
        step_y(cot_y)

    turned_x = [Held(jnp.stack([t.value for t in turned]))]
    line = [Held(jnp.concatenate([part.value, turned_part.value], axis=0))]
    line.append(lane_z.send(line[-1], ring_z))
    turned_x.append(lane_x.send(turned_x[-1], ring_x))
    far = [Held(wide.value)]
    line.append(lane_z.send(line[-1], ring_z))
    turned_x.append(lane_x.send(turned_x[-1], ring_x))
    far_wide = lane_z.send(far[0], swap_half)
    line.append(lane_z.send(line[-1], ring_z))
    turned_x.append(lane_x.send(turned_x[-1], ring_x))
    far_k = [far_wide]

    line_y = [None] + [[line[s]] for s in range(1, nz)]
    for _ in range(ny - 1):
        step_y(line_y[1])
        step_y(line_y[2])
    for _ in range(nx - 1):
        far_k.append(lane_x.send(far_k[-1], ring_x))

    def placed(blocks, position, count, pick=lambda v: v):
        first = pick(blocks[0].value)
        whole = jnp.zeros((count,) + first.shape, first.dtype)
        for step, block in enumerate(blocks):
            whole = lax.dynamic_update_index_in_dim(
                whole, pick(block.value), (position - step * way) % count, 0
            )
        return whole

    cot_own = placed(cot_y, y, ny)
    cot_own = cot_own.reshape(ny, nz, rows, -1)
    lined = jnp.zeros((nz, ny, rows, cotangent.shape[1]), bf16)
    for s in range(nz):
        lined = lax.dynamic_update_index_in_dim(lined, cot_own[:, s], (zlo - s * way) % nz, 0)
    lined = Held(lined.reshape(nz * ny * rows, -1))
    lined_other = lane_core.send(lined, swap_core)
    token_rows = placed(turned_x, x, nx)
    grad = 0.0
    for co, block in ((core, lined), (1 - core, lined_other)):
        picked = lax.dynamic_index_in_dim(token_rows, (zhi + co) % 2, 1, keepdims=False)
        grad += lax.dot_general(
            picked.reshape(nx * ny * rows, -1),
            block.value,
            (((0,), (0,)), ((), ())),
            preferred_element_type=f32,
        )
    grad = grad * grad_scale
    new_first = beta_one * first_moment + (1.0 - beta_one) * grad
    new_second = beta_two * second_moment + (1.0 - beta_two) * grad * grad
    step_value = new_first / bias_one / (jnp.sqrt(new_second / bias_two) + adam_eps)
    new_master = master - learn_rate * (step_value + decay_rate * master)

    fresh = [Held(new_master.astype(bf16))]
    for _ in range(ny - 1):
        step_y(line_y[3])
        step_y(fresh)
    new_weight = placed(fresh, y, ny).reshape(weight.shape)

    own = placed(own_k, x, nx)
    across = placed(far_k, x, nx)
    queries = 0.0
    token_grad = 0.0
    for s in range(nz):
        if s == 0:
            plain = Held(weight)
            turn_full = Held(placed(turned_y, y, ny).reshape(weight.shape))
        else:
            plain = Held(placed(line_y[s], y, ny, lambda v: v[:quarter]).reshape(weight.shape))
            turn_full = Held(placed(line_y[s], y, ny, lambda v: v[quarter:]).reshape(weight.shape))
        plain_other = lane_core.send(plain, swap_core)
        turn_other = lane_core.send(turn_full, swap_core)
        for co, sign, one, two in (
            (core, 1, plain, turn_full),
            (1 - core, -1, plain_other, turn_other),
        ):
            zl = (zlo - s * sign * way) % nz
            block = jnp.where(
                zhi == co,
                lax.dynamic_index_in_dim(own, zl, 0, keepdims=False),
                lax.dynamic_index_in_dim(across, zl, 0, keepdims=False),
            )
            queries += jnp.dot(block[:, :features], one.value, preferred_element_type=f32)
            token_grad += lax.dot_general(
                block[:, features:], two.value, (((1,), (1,)), ((), ())), preferred_element_type=f32
            )
    return (
        queries.astype(bf16),
        token_grad.astype(bf16),
        new_master,
        new_first,
        new_second,
        new_weight,
    )


def solution(mesh):
    in_specs = (
        P(("row", "depth"), "col"),
        P("row", "col"),
        P(("row", "depth"), "col"),
        P(("row", "depth"), "col"),
        P(("row", "depth"), "col"),
        P(("row", "depth"), "col"),
    )
    out_specs = (
        P(("row", "depth"), "col"),
        P(("row", "depth"), "col"),
        P(("row", "depth"), "col"),
        P(("row", "depth"), "col"),
        P(("row", "depth"), "col"),
        P("row", "col"),
    )
    return jax.shard_map(local, mesh=mesh, in_specs=in_specs, out_specs=out_specs, check_vma=False)
```

```python
import math

import jax
import jax.numpy as jnp
from jax import lax
from jax.sharding import PartitionSpec as P

beta_one = 0.9
beta_two = 0.95
learn_rate = 0.02
decay_rate = 0.1
adam_eps = 1e-08
bias_one = 1.0 - 0.9**50
bias_two = 1.0 - 0.95**50

AXES = ("row", "col", "depth")
f32 = jnp.float32
bf16 = jnp.bfloat16


def moves(sizes, change):
    rows, cols, depths = sizes
    pairs = []
    for r in range(rows):
        for c in range(cols):
            for y in range(depths):
                zlo, core, x, zhi, yy = change(r // 2, r % 2, c // 2, c % 2, y)
                pairs.append(
                    (
                        (r * cols + c) * depths + y,
                        ((zlo * 2 + core) * cols + x * 2 + zhi) * depths + yy,
                    )
                )
    return pairs


class Held:
    def __init__(self, value):
        self.value = value


def hold(*helds):
    unique = list({id(h): h for h in helds}.values())
    for h, v in zip(unique, lax.optimization_barrier(tuple(h.value for h in unique))):
        h.value = v


class Lane:
    def __init__(self, lag):
        self.lag = lag
        self.past = []

    def send(self, held, pairs, after=()):
        before = self.past[-self.lag :][:1] if len(self.past) >= self.lag else []
        if before or after:
            hold(held, *before, *after)
        out = Held(lax.ppermute(held.value, AXES, pairs))
        self.past.append(out)
        return out


def local(tokens, weight, cotangent, master, first_moment, second_moment):
    sizes = tuple(lax.axis_size(a) for a in AXES)
    nz, nx, ny = sizes[0] // 2, sizes[1] // 2, sizes[2]
    total_tokens = tokens.shape[0] * sizes[0] * sizes[2]
    grad_scale = 1.0 / math.sqrt(total_tokens)
    row, col, y = (lax.axis_index(a) for a in AXES)
    zlo, core, x, zhi = row // 2, row % 2, col // 2, col % 2
    way = 1 - 2 * core

    def pairs(change):
        return moves(sizes, change)

    ring_x = pairs(lambda zl, co, xx, zh, yy: (zl, co, (xx + 1 - 2 * co) % nx, zh, yy))
    ring_y = pairs(lambda zl, co, xx, zh, yy: (zl, co, xx, zh, (yy + 1 - 2 * co) % ny))
    ring_z = pairs(lambda zl, co, xx, zh, yy: ((zl + 1 - 2 * co) % nz, co, xx, zh, yy))
    turn = pairs(lambda zl, co, xx, zh, yy: (xx, zh, zl, co, yy))
    turn_near = pairs(lambda zl, co, xx, zh, yy: (xx, zh, (xx + zl) % nx, co, yy))
    turn_far = pairs(lambda zl, co, xx, zh, yy: (xx, zh, (xx + zl) % nx, 1 - co, yy))
    far_y = [
        pairs(lambda zl, co, xx, zh, yy: (zl, co, xx, zh, (yy + s * (1 - 2 * co)) % ny))
        for s in range(1, ny)
    ]
    swap_core = pairs(lambda zl, co, xx, zh, yy: (zl, 1 - co, xx, zh, yy))
    swap_half = pairs(lambda zl, co, xx, zh, yy: (zl, co, xx, 1 - zh, yy))

    lane_x, lane_y, lane_z, lane_core = Lane(2), Lane(2), Lane(2), Lane(2)

    quarter = weight.shape[0] // ny
    rows = cotangent.shape[0]
    features = tokens.shape[1]
    part = Held(lax.dynamic_slice_in_dim(weight, y * quarter, quarter, 0))
    wide = Held(jnp.concatenate([tokens, cotangent], axis=1))
    token_block = Held(tokens)
    cot_block = Held(cotangent)
    spread = Held(lax.all_to_all(tokens, "depth", 1, 0, tiled=True))

    own_k = [wide]
    turned_part = lane_z.send(part, turn)
    cot_line = [cot_block]
    cot_line.append(lane_z.send(cot_line[-1], ring_z))
    own_k.append(lane_x.send(own_k[-1], ring_x))
    turned = [lane_z.send(spread, turn_near)]
    cot_line.append(lane_z.send(cot_line[-1], ring_z))
    own_k.append(lane_x.send(own_k[-1], ring_x))
    turned.append(lane_z.send(spread, turn_far))
    cot_line.append(lane_z.send(cot_line[-1], ring_z))
    own_k.append(lane_x.send(own_k[-1], ring_x))
    line = [Held(jnp.concatenate([part.value, turned_part.value], axis=0))]
    line.append(lane_z.send(line[-1], ring_z))

    def gather_y(held):
        return [held]

    def step_y(blocks, after=()):
        blocks.append(lane_y.send(blocks[-1], ring_y, after))

    turned_y = [turned_part]
    cot_y = [Held(jnp.concatenate([c.value for c in cot_line], axis=0))]
    for _ in range(ny - 1):
        step_y(turned_y)
        step_y(cot_y)

    turned_x = [Held(jnp.stack([t.value for t in turned]))]
    turned_x.append(lane_x.send(turned_x[-1], ring_x))
    far = [Held(wide.value)]
    line.append(lane_z.send(line[-1], ring_z))
    turned_x.append(lane_x.send(turned_x[-1], ring_x))
    far_wide = lane_z.send(far[0], swap_half)
    line.append(lane_z.send(line[-1], ring_z))
    turned_x.append(lane_x.send(turned_x[-1], ring_x))
    far_k = [far_wide]

    line_y = [None] + [[line[s]] for s in range(1, nz)]
    for _ in range(ny - 1):
        step_y(line_y[1])
        step_y(line_y[2])
    for _ in range(nx - 1):
        far_k.append(lane_x.send(far_k[-1], ring_x))

    def placed(blocks, position, count, pick=lambda v: v):
        first = pick(blocks[0].value)
        whole = jnp.zeros((count,) + first.shape, first.dtype)
        for step, block in enumerate(blocks):
            whole = lax.dynamic_update_index_in_dim(
                whole, pick(block.value), (position - step * way) % count, 0
            )
        return whole

    cot_own = placed(cot_y, y, ny)
    cot_own = cot_own.reshape(ny, nz, rows, -1)
    lined = jnp.zeros((nz, ny, rows, cotangent.shape[1]), bf16)
    for s in range(nz):
        lined = lax.dynamic_update_index_in_dim(lined, cot_own[:, s], (zlo - s * way) % nz, 0)
    lined = Held(lined.reshape(nz * ny * rows, -1))
    lined_other = lane_core.send(lined, swap_core)
    token_rows = placed(turned_x, x - zlo, nx)
    grad = 0.0
    for co, block in ((core, lined), (1 - core, lined_other)):
        picked = lax.dynamic_index_in_dim(token_rows, (zhi + co) % 2, 1, keepdims=False)
        grad += lax.dot_general(
            picked.reshape(nx * ny * rows, -1),
            block.value,
            (((0,), (0,)), ((), ())),
            preferred_element_type=f32,
        )
    grad = grad * grad_scale
    new_first = beta_one * first_moment + (1.0 - beta_one) * grad
    new_second = beta_two * second_moment + (1.0 - beta_two) * grad * grad
    step_value = new_first / bias_one / (jnp.sqrt(new_second / bias_two) + adam_eps)
    new_master = master - learn_rate * (step_value + decay_rate * master)

    fresh = [Held(new_master.astype(bf16))]
    for k in range(ny - 1):
        step_y(line_y[3], (fresh[0],) if k == 2 else ())
        step_y(fresh)
    new_weight = placed(fresh, y, ny).reshape(weight.shape)

    own = placed(own_k, x, nx)
    across = placed(far_k, x, nx)
    queries = 0.0
    token_grad = 0.0
    for s in range(nz):
        if s == 0:
            plain = Held(weight)
            turn_full = Held(placed(turned_y, y, ny).reshape(weight.shape))
        else:
            plain = Held(placed(line_y[s], y, ny, lambda v: v[:quarter]).reshape(weight.shape))
            turn_full = Held(placed(line_y[s], y, ny, lambda v: v[quarter:]).reshape(weight.shape))
        plain_other = lane_core.send(plain, swap_core)
        turn_other = lane_core.send(turn_full, swap_core)
        for co, sign, one, two in (
            (core, 1, plain, turn_full),
            (1 - core, -1, plain_other, turn_other),
        ):
            zl = (zlo - s * sign * way) % nz
            block = jnp.where(
                zhi == co,
                lax.dynamic_index_in_dim(own, zl, 0, keepdims=False),
                lax.dynamic_index_in_dim(across, zl, 0, keepdims=False),
            )
            queries += jnp.dot(block[:, :features], one.value, preferred_element_type=f32)
            token_grad += lax.dot_general(
                block[:, features:], two.value, (((1,), (1,)), ((), ())), preferred_element_type=f32
            )
    return (
        queries.astype(bf16),
        token_grad.astype(bf16),
        new_master,
        new_first,
        new_second,
        new_weight,
    )


def solution(mesh):
    in_specs = (
        P(("row", "depth"), "col"),
        P("row", "col"),
        P(("row", "depth"), "col"),
        P(("row", "depth"), "col"),
        P(("row", "depth"), "col"),
        P(("row", "depth"), "col"),
    )
    out_specs = (
        P(("row", "depth"), "col"),
        P(("row", "depth"), "col"),
        P(("row", "depth"), "col"),
        P(("row", "depth"), "col"),
        P(("row", "depth"), "col"),
        P("row", "col"),
    )
    return jax.shard_map(local, mesh=mesh, in_specs=in_specs, out_specs=out_specs, check_vma=False)
```

```python
import math

import jax
import jax.numpy as jnp
from jax import lax
from jax.sharding import PartitionSpec as P

beta_one = 0.9
beta_two = 0.95
learn_rate = 0.02
decay_rate = 0.1
adam_eps = 1e-08
bias_one = 1.0 - 0.9**50
bias_two = 1.0 - 0.95**50

AXES = ("row", "col", "depth")
f32 = jnp.float32
bf16 = jnp.bfloat16


def moves(sizes, change):
    rows, cols, depths = sizes
    pairs = []
    for r in range(rows):
        for c in range(cols):
            for y in range(depths):
                zlo, core, x, zhi, yy = change(r // 2, r % 2, c // 2, c % 2, y)
                pairs.append(
                    (
                        (r * cols + c) * depths + y,
                        ((zlo * 2 + core) * cols + x * 2 + zhi) * depths + yy,
                    )
                )
    return pairs


class Held:
    def __init__(self, value):
        self.value = value


def hold(*helds):
    unique = list({id(h): h for h in helds}.values())
    for h, v in zip(unique, lax.optimization_barrier(tuple(h.value for h in unique))):
        h.value = v


class Lane:
    def __init__(self, lag):
        self.lag = lag
        self.past = []

    def send(self, held, pairs, after=()):
        before = self.past[-self.lag :][:1] if len(self.past) >= self.lag else []
        if before or after:
            hold(held, *before, *after)
        out = Held(lax.ppermute(held.value, AXES, pairs))
        self.past.append(out)
        return out


def local(tokens, weight, cotangent, master, first_moment, second_moment):
    sizes = tuple(lax.axis_size(a) for a in AXES)
    nz, nx, ny = sizes[0] // 2, sizes[1] // 2, sizes[2]
    total_tokens = tokens.shape[0] * sizes[0] * sizes[2]
    grad_scale = 1.0 / math.sqrt(total_tokens)
    row, col, y = (lax.axis_index(a) for a in AXES)
    zlo, core, x, zhi = row // 2, row % 2, col // 2, col % 2
    way = 1 - 2 * core

    def pairs(change):
        return moves(sizes, change)

    ring_x = pairs(lambda zl, co, xx, zh, yy: (zl, co, (xx + 1 - 2 * co) % nx, zh, yy))
    ring_y = pairs(lambda zl, co, xx, zh, yy: (zl, co, xx, zh, (yy + 1 - 2 * co) % ny))
    ring_z = pairs(lambda zl, co, xx, zh, yy: ((zl + 1 - 2 * co) % nz, co, xx, zh, yy))
    turn = pairs(lambda zl, co, xx, zh, yy: (xx, zh, zl, co, yy))
    turn_near = pairs(lambda zl, co, xx, zh, yy: (xx, zh, (xx + zl) % nx, co, yy))
    turn_far = pairs(lambda zl, co, xx, zh, yy: (xx, zh, (xx + zl) % nx, 1 - co, yy))
    far_y = [
        pairs(lambda zl, co, xx, zh, yy: (zl, co, xx, zh, (yy + s * (1 - 2 * co)) % ny))
        for s in range(1, ny)
    ]
    swap_core = pairs(lambda zl, co, xx, zh, yy: (zl, 1 - co, xx, zh, yy))
    swap_half = pairs(lambda zl, co, xx, zh, yy: (zl, co, xx, 1 - zh, yy))

    lane_x, lane_y, lane_z, lane_core = Lane(2), Lane(2), Lane(2), Lane(2)

    quarter = weight.shape[0] // ny
    rows = cotangent.shape[0]
    features = tokens.shape[1]
    part = Held(lax.dynamic_slice_in_dim(weight, y * quarter, quarter, 0))
    wide = Held(jnp.concatenate([tokens, cotangent], axis=1))
    token_block = Held(tokens)
    cot_block = Held(cotangent)
    spread = Held(lax.all_to_all(tokens, "depth", 1, 0, tiled=True))

    own_k = [wide]
    turned_part = lane_z.send(part, turn)
    cot_line = [cot_block]
    cot_line.append(lane_z.send(cot_line[-1], ring_z))
    own_k.append(lane_x.send(own_k[-1], ring_x))
    cot_line.append(lane_z.send(cot_line[-1], ring_z))
    turned = [lane_z.send(spread, turn_near)]
    own_k.append(lane_x.send(own_k[-1], ring_x))
    cot_line.append(lane_z.send(cot_line[-1], ring_z))
    line = [Held(jnp.concatenate([part.value, turned_part.value], axis=0))]
    line.append(lane_z.send(line[-1], ring_z))
    turned.append(lane_z.send(spread, turn_far))
    own_k.append(lane_x.send(own_k[-1], ring_x))

    def gather_y(held):
        return [held]

    def step_y(blocks, after=()):
        blocks.append(lane_y.send(blocks[-1], ring_y, after))

    turned_y = [turned_part]
    cot_y = [Held(jnp.concatenate([c.value for c in cot_line], axis=0))]
    for _ in range(ny - 1):
        step_y(turned_y)
        step_y(cot_y)

    turned_x = [Held(jnp.stack([t.value for t in turned]))]
    turned_x.append(lane_x.send(turned_x[-1], ring_x))
    far = [Held(wide.value)]
    line.append(lane_z.send(line[-1], ring_z))
    turned_x.append(lane_x.send(turned_x[-1], ring_x))
    far_wide = lane_z.send(far[0], swap_half)
    line.append(lane_z.send(line[-1], ring_z))
    turned_x.append(lane_x.send(turned_x[-1], ring_x))
    far_k = [far_wide]

    line_y = [None] + [[line[s]] for s in range(1, nz)]
    for _ in range(ny - 1):
        step_y(line_y[1])
        step_y(line_y[2])
    for _ in range(nx - 1):
        far_k.append(lane_x.send(far_k[-1], ring_x))

    def placed(blocks, position, count, pick=lambda v: v):
        first = pick(blocks[0].value)
        whole = jnp.zeros((count,) + first.shape, first.dtype)
        for step, block in enumerate(blocks):
            whole = lax.dynamic_update_index_in_dim(
                whole, pick(block.value), (position - step * way) % count, 0
            )
        return whole

    cot_own = placed(cot_y, y, ny)
    cot_own = cot_own.reshape(ny, nz, rows, -1)
    lined = jnp.zeros((nz, ny, rows, cotangent.shape[1]), bf16)
    for s in range(nz):
        lined = lax.dynamic_update_index_in_dim(lined, cot_own[:, s], (zlo - s * way) % nz, 0)
    lined = Held(lined.reshape(nz * ny * rows, -1))
    lined_other = lane_core.send(lined, swap_core)
    token_rows = placed(turned_x, x - zlo, nx)
    grad = 0.0
    for co, block in ((core, lined), (1 - core, lined_other)):
        picked = lax.dynamic_index_in_dim(token_rows, (zhi + co) % 2, 1, keepdims=False)
        grad += lax.dot_general(
            picked.reshape(nx * ny * rows, -1),
            block.value,
            (((0,), (0,)), ((), ())),
            preferred_element_type=f32,
        )
    grad = grad * grad_scale
    new_first = beta_one * first_moment + (1.0 - beta_one) * grad
    new_second = beta_two * second_moment + (1.0 - beta_two) * grad * grad
    step_value = new_first / bias_one / (jnp.sqrt(new_second / bias_two) + adam_eps)
    new_master = master - learn_rate * (step_value + decay_rate * master)

    fresh = [Held(new_master.astype(bf16))]
    for k in range(ny - 1):
        step_y(line_y[3], (fresh[0],) if k == 2 else ())
        step_y(fresh)
    new_weight = placed(fresh, y, ny).reshape(weight.shape)

    own = placed(own_k, x, nx)
    across = placed(far_k, x, nx)
    queries = 0.0
    token_grad = 0.0
    for s in range(nz):
        if s == 0:
            plain = Held(weight)
            hold(plain, line_y[1][-1])
            turn_full = Held(placed(turned_y, y, ny).reshape(weight.shape))
        else:
            plain = Held(placed(line_y[s], y, ny, lambda v: v[:quarter]).reshape(weight.shape))
            turn_full = Held(placed(line_y[s], y, ny, lambda v: v[quarter:]).reshape(weight.shape))
        plain_other = lane_core.send(plain, swap_core)
        turn_other = lane_core.send(turn_full, swap_core)
        for co, sign, one, two in (
            (core, 1, plain, turn_full),
            (1 - core, -1, plain_other, turn_other),
        ):
            zl = (zlo - s * sign * way) % nz
            block = jnp.where(
                zhi == co,
                lax.dynamic_index_in_dim(own, zl, 0, keepdims=False),
                lax.dynamic_index_in_dim(across, zl, 0, keepdims=False),
            )
            queries += jnp.dot(block[:, :features], one.value, preferred_element_type=f32)
            token_grad += lax.dot_general(
                block[:, features:], two.value, (((1,), (1,)), ((), ())), preferred_element_type=f32
            )
    return (
        queries.astype(bf16),
        token_grad.astype(bf16),
        new_master,
        new_first,
        new_second,
        new_weight,
    )


def solution(mesh):
    in_specs = (
        P(("row", "depth"), "col"),
        P("row", "col"),
        P(("row", "depth"), "col"),
        P(("row", "depth"), "col"),
        P(("row", "depth"), "col"),
        P(("row", "depth"), "col"),
    )
    out_specs = (
        P(("row", "depth"), "col"),
        P(("row", "depth"), "col"),
        P(("row", "depth"), "col"),
        P(("row", "depth"), "col"),
        P(("row", "depth"), "col"),
        P("row", "col"),
    )
    return jax.shard_map(local, mesh=mesh, in_specs=in_specs, out_specs=out_specs, check_vma=False)
```

```python
import math

import jax
import jax.numpy as jnp
from jax import lax
from jax.sharding import PartitionSpec as P

beta_one = 0.9
beta_two = 0.95
learn_rate = 0.02
decay_rate = 0.1
adam_eps = 1e-08
bias_one = 1.0 - 0.9**50
bias_two = 1.0 - 0.95**50

AXES = ("row", "col", "depth")
f32 = jnp.float32
bf16 = jnp.bfloat16


def moves(sizes, change):
    rows, cols, depths = sizes
    pairs = []
    for r in range(rows):
        for c in range(cols):
            for y in range(depths):
                zlo, core, x, zhi, yy = change(r // 2, r % 2, c // 2, c % 2, y)
                pairs.append(
                    (
                        (r * cols + c) * depths + y,
                        ((zlo * 2 + core) * cols + x * 2 + zhi) * depths + yy,
                    )
                )
    return pairs


class Held:
    def __init__(self, value):
        self.value = value


def hold(*helds):
    unique = list({id(h): h for h in helds}.values())
    for h, v in zip(unique, lax.optimization_barrier(tuple(h.value for h in unique))):
        h.value = v


class Lane:
    def __init__(self, lag):
        self.lag = lag
        self.past = []

    def send(self, held, pairs, after=()):
        before = self.past[-self.lag :][:1] if len(self.past) >= self.lag else []
        if before or after:
            hold(held, *before, *after)
        out = Held(lax.ppermute(held.value, AXES, pairs))
        self.past.append(out)
        return out


def local(tokens, weight, cotangent, master, first_moment, second_moment):
    sizes = tuple(lax.axis_size(a) for a in AXES)
    nz, nx, ny = sizes[0] // 2, sizes[1] // 2, sizes[2]
    total_tokens = tokens.shape[0] * sizes[0] * sizes[2]
    grad_scale = 1.0 / math.sqrt(total_tokens)
    row, col, y = (lax.axis_index(a) for a in AXES)
    zlo, core, x, zhi = row // 2, row % 2, col // 2, col % 2
    way = 1 - 2 * core

    def pairs(change):
        return moves(sizes, change)

    ring_x = pairs(lambda zl, co, xx, zh, yy: (zl, co, (xx + 1 - 2 * co) % nx, zh, yy))
    ring_y = pairs(lambda zl, co, xx, zh, yy: (zl, co, xx, zh, (yy + 1 - 2 * co) % ny))
    ring_z = pairs(lambda zl, co, xx, zh, yy: ((zl + 1 - 2 * co) % nz, co, xx, zh, yy))
    turn = pairs(lambda zl, co, xx, zh, yy: (xx, zh, zl, co, yy))
    turn_near = pairs(lambda zl, co, xx, zh, yy: (xx, zh, (xx + zl) % nx, co, yy))
    turn_far = pairs(lambda zl, co, xx, zh, yy: (xx, zh, (xx + zl) % nx, 1 - co, yy))
    far_y = [
        pairs(lambda zl, co, xx, zh, yy: (zl, co, xx, zh, (yy + s * (1 - 2 * co)) % ny))
        for s in range(1, ny)
    ]
    swap_core = pairs(lambda zl, co, xx, zh, yy: (zl, 1 - co, xx, zh, yy))
    swap_half = pairs(lambda zl, co, xx, zh, yy: (zl, co, xx, 1 - zh, yy))

    lane_x, lane_y, lane_z, lane_core = Lane(2), Lane(2), Lane(2), Lane(2)

    quarter = weight.shape[0] // ny
    rows = cotangent.shape[0]
    features = tokens.shape[1]
    part = Held(lax.dynamic_slice_in_dim(weight, y * quarter, quarter, 0))
    wide = Held(jnp.concatenate([tokens, cotangent], axis=1))
    token_block = Held(tokens)
    cot_block = Held(cotangent)
    spread = Held(lax.all_to_all(tokens, "depth", 1, 0, tiled=True))

    own_k = [wide]
    turned_part = lane_z.send(part, turn)
    cot_line = [cot_block]
    cot_line.append(lane_z.send(cot_line[-1], ring_z))
    own_k.append(lane_x.send(own_k[-1], ring_x))
    cot_line.append(lane_z.send(cot_line[-1], ring_z))
    turned = [lane_z.send(spread, turn_near)]
    own_k.append(lane_x.send(own_k[-1], ring_x))
    cot_line.append(lane_z.send(cot_line[-1], ring_z))
    line = [Held(jnp.concatenate([part.value, turned_part.value], axis=0))]
    line.append(lane_z.send(line[-1], ring_z))
    turned.append(lane_z.send(spread, turn_far))
    own_k.append(lane_x.send(own_k[-1], ring_x))

    def gather_y(held):
        return [held]

    def step_y(blocks, after=()):
        blocks.append(lane_y.send(blocks[-1], ring_y, after))

    turned_y = [turned_part]
    cot_y = [Held(jnp.concatenate([c.value for c in cot_line], axis=0))]
    for _ in range(ny - 1):
        step_y(turned_y)
        step_y(cot_y)

    turned_x = [Held(jnp.stack([t.value for t in turned]))]
    turned_x.append(lane_x.send(turned_x[-1], ring_x))
    far = [Held(wide.value)]
    line.append(lane_z.send(line[-1], ring_z))
    turned_x.append(lane_x.send(turned_x[-1], ring_x))
    far_wide = lane_z.send(far[0], swap_half)
    line.append(lane_z.send(line[-1], ring_z))
    turned_x.append(lane_x.send(turned_x[-1], ring_x))
    far_k = [far_wide]

    line_y = [None] + [[line[s]] for s in range(1, nz)]
    for _ in range(ny - 1):
        step_y(line_y[1])
        step_y(line_y[2])
    for _ in range(nx - 1):
        far_k.append(lane_x.send(far_k[-1], ring_x))

    def placed(blocks, position, count, pick=lambda v: v):
        first = pick(blocks[0].value)
        whole = jnp.zeros((count,) + first.shape, first.dtype)
        for step, block in enumerate(blocks):
            whole = lax.dynamic_update_index_in_dim(
                whole, pick(block.value), (position - step * way) % count, 0
            )
        return whole

    cot_own = placed(cot_y, y, ny)
    cot_own = cot_own.reshape(ny, nz, rows, -1)
    lined = jnp.zeros((nz, ny, rows, cotangent.shape[1]), bf16)
    for s in range(nz):
        lined = lax.dynamic_update_index_in_dim(lined, cot_own[:, s], (zlo - s * way) % nz, 0)
    lined = Held(lined.reshape(nz * ny * rows, -1))
    lined_other = lane_core.send(lined, swap_core)
    token_rows = placed(turned_x, x - zlo, nx)
    grad = 0.0
    for co, block in ((core, lined), (1 - core, lined_other)):
        picked = lax.dynamic_index_in_dim(token_rows, (zhi + co) % 2, 1, keepdims=False)
        grad += lax.dot_general(
            picked.reshape(nx * ny * rows, -1),
            block.value,
            (((0,), (0,)), ((), ())),
            preferred_element_type=f32,
        )
    grad = grad * grad_scale
    new_first = beta_one * first_moment + (1.0 - beta_one) * grad
    new_second = beta_two * second_moment + (1.0 - beta_two) * grad * grad
    step_value = new_first / bias_one / (jnp.sqrt(new_second / bias_two) + adam_eps)
    new_master = master - learn_rate * (step_value + decay_rate * master)

    fresh = [Held(new_master.astype(bf16))]
    for k in range(ny - 1):
        step_y(line_y[3], (fresh[0],) if k == 2 else ())
        fresh.append(lane_y.send(fresh[0], far_y[k]))
    new_weight = placed(fresh, y, ny).reshape(weight.shape)

    own = placed(own_k, x, nx)
    across = placed(far_k, x, nx)
    queries = 0.0
    token_grad = 0.0
    for s in range(nz):
        if s == 0:
            plain = Held(weight)
            hold(plain, line_y[1][-1])
            turn_full = Held(placed(turned_y, y, ny).reshape(weight.shape))
        else:
            plain = Held(placed(line_y[s], y, ny, lambda v: v[:quarter]).reshape(weight.shape))
            turn_full = Held(placed(line_y[s], y, ny, lambda v: v[quarter:]).reshape(weight.shape))
        plain_other = lane_core.send(plain, swap_core)
        turn_other = lane_core.send(turn_full, swap_core)
        for co, sign, one, two in (
            (core, 1, plain, turn_full),
            (1 - core, -1, plain_other, turn_other),
        ):
            zl = (zlo - s * sign * way) % nz
            block = jnp.where(
                zhi == co,
                lax.dynamic_index_in_dim(own, zl, 0, keepdims=False),
                lax.dynamic_index_in_dim(across, zl, 0, keepdims=False),
            )
            queries += jnp.dot(block[:, :features], one.value, preferred_element_type=f32)
            token_grad += lax.dot_general(
                block[:, features:], two.value, (((1,), (1,)), ((), ())), preferred_element_type=f32
            )
    return (
        queries.astype(bf16),
        token_grad.astype(bf16),
        new_master,
        new_first,
        new_second,
        new_weight,
    )


def solution(mesh):
    in_specs = (
        P(("row", "depth"), "col"),
        P("row", "col"),
        P(("row", "depth"), "col"),
        P(("row", "depth"), "col"),
        P(("row", "depth"), "col"),
        P(("row", "depth"), "col"),
    )
    out_specs = (
        P(("row", "depth"), "col"),
        P(("row", "depth"), "col"),
        P(("row", "depth"), "col"),
        P(("row", "depth"), "col"),
        P(("row", "depth"), "col"),
        P("row", "col"),
    )
    return jax.shard_map(local, mesh=mesh, in_specs=in_specs, out_specs=out_specs, check_vma=False)
```
